512 devices in a mesh: row: 64 (over x, y, core), col: 8 (over z).
Axes of the slice: x: 4, y: 8, z: 8, core: 2. Of those that a mesh axis runs over, the one named last changes fastest.
Arguments:
- right_sides: float32 [16, 2048, 1024], P(None, 'row', 'col'), may hold values from -6 to 6
- first_panel: float32 [15, 2048, 2048], P(None, 'row', 'col'), may hold values from -0.125 to 0.125
- second_panel: float32 [14, 2048, 2048], P(None, 'row', 'col'), may hold values from -0.125 to 0.125
- inverse_transposed: float32 [2, 2048, 2048], P(None, 'row', 'col'), as said below
Outputs:
- solution: float32 [2, 2048, 1024], P(None, 'col')
- remaining: float32 [14, 2048, 1024], P(None, 'row', 'col')
The draws below stay inside these ranges and needn't reach their ends.
Inputs may be any that keep to these rules, and one draw needn't show every extreme that they name: inverse_transposed[k, s, x] is zero where s > x (each block is the transpose of a lower triangular inverse).
All inputs are finite; a program needn't handle non-finite values.
Results may differ from the reference program's by a relative error of at most 0.000094.
Values sent between devices are 32-bit elements; how exact they have to be, the bound alone decides.
A program may use at most 64 MiB of HBM per device.

```python
import math
import jax
import jax.numpy as jnp
from jax import lax

NB = 2048
NRHS = 1024
BLOCKS = 16


def draw_inverse_transposed(key, part):
    key = jax.random.fold_in(key, 5)
    diag_key, off_key = jax.random.split(key)
    off_terms = jax.random.normal(off_key, (2, NB, NB), jnp.float32) / NB ** 0.5
    diag_terms = jnp.exp(jax.random.uniform(diag_key, (2, NB, 1), jnp.float32, math.log(0.5), math.log(2.0)))
    source = lax.broadcasted_iota(jnp.int32, (2, NB, NB), 1)
    target = lax.broadcasted_iota(jnp.int32, (2, NB, NB), 2)
    return jnp.where(source < target, off_terms, 0.0) + jnp.where(source == target, diag_terms, 0.0)


def shard_levels(stream_key, dims, pieces, smallest, top_value):
    factor_of = 1.0
    for axis_at, blocks in pieces:
        heights = jax.random.uniform(jax.random.fold_in(jax.random.fold_in(stream_key, 6), axis_at), (blocks,), jnp.float32, smallest / len(pieces), top_value / len(pieces))
        factor_of = factor_of * jnp.repeat(jnp.exp(heights), dims[axis_at] // blocks).reshape((-1,) + (1,) * (len(dims) - 1 - axis_at))
    return factor_of


def bell_draw(rng, dims, width, limit, shards=(), dtype=jnp.bfloat16):
    entries = jax.random.normal(rng, dims, jnp.float32) * width
    if len(shards) > 0:
        entries = shard_levels(rng, dims, shards, -0.22, 0.18) * entries
    return jnp.clip(entries, min=-limit, max=limit).astype(dtype)


def setup_inputs(seed: int = 0) -> dict:
    arg_keys = jax.random.split(jax.random.key(seed), 5)
    right_sides = bell_draw(arg_keys[0], (BLOCKS, NB, NRHS), 1.0, 6.0, ((1, 64), (2, 8)), jnp.float32)
    first_panel = bell_draw(arg_keys[1], (BLOCKS - 1, NB, NB), NB ** -0.5, 0.125, ((1, 64), (2, 8)), jnp.float32)
    second_panel = bell_draw(arg_keys[2], (BLOCKS - 2, NB, NB), NB ** -0.5, 0.125, ((1, 64), (2, 8)), jnp.float32)
    inverse_transposed = draw_inverse_transposed(jax.random.fold_in(arg_keys[4], 71), 0)
    return dict(right_sides=right_sides, first_panel=first_panel, second_panel=second_panel, inverse_transposed=inverse_transposed)


def solve_block(inverse_t, rows):
    return lax.dot_general(inverse_t, rows, (((0,), (0,)), ((), ())), precision=lax.Precision.HIGHEST, preferred_element_type=jnp.float32)


def apply_panel(panel, solved):
    return jnp.einsum("bij,jk->bik", panel, solved, precision=lax.Precision.HIGHEST)


def reference(right_sides, first_panel, second_panel, inverse_transposed):
    first = solve_block(inverse_transposed[0], right_sides[0])
    updated = right_sides[1:] - apply_panel(first_panel, first)
    second = solve_block(inverse_transposed[1], updated[0])
    remaining = updated[1:] - apply_panel(second_panel, second)
    solution = jnp.stack([first, second])
    return solution, remaining
```

```python
import functools

import jax
import jax.numpy as jnp
from jax import lax
from jax.experimental import pallas as pl
from jax.experimental.pallas import tpu as pltpu
from jax.sharding import PartitionSpec as P

MESH = pl.DeviceIdType.MESH
F32 = jnp.float32
BF16 = jnp.bfloat16

NEAR = (1, 7, 2, 6, 3, 5, 4)
FAR = NEAR[::-1]
GROUP = ((2, 0), (2, 1), (1, 0), (3, 0), (1, 1), (3, 1), (0, 1))


def split(a):
    hi = a.astype(BF16)
    return hi, (a - hi.astype(F32)).astype(BF16)


def dot(a, b):
    return jnp.dot(a, b, preferred_element_type=F32)


def dot3(a, b):
    (ah, al), (bh, bl) = a, b
    return dot(ah, bh) + (dot(al, bh) + dot(ah, bl))


def kernel(
    rhs, pan1, pan2, inv, sol, rem,
    rz, r, m0, m1, m2, r1t, pa, pa_in, pb, pb_in, u, pc, pc_in,
    full, acc, p1h, p1l, p2h, p2l, ring1, ring2,
    s_rz, q_rz, s_m, q_m, s_r1, q_r1, s_r, q_r, s_a, q_a, s_f, q_f, s_fx, q_fx, s_fc, q_fc,
    s_b, q_b, s_u, q_u, s_c, q_c, s_s, q_s, s_sx, q_sx, s_sc, q_sc, s_1, q_1, s_2, q_2,
):
    row = lax.axis_index("row")
    c = lax.axis_index("col")
    x, y, q = row // 16, (row // 2) % 8, row % 2
    g = 2 * x + q

    def dev(gg, yy, cc):
        return (((gg // 2) * 8 + yy) * 2 + gg % 2, cc)

    def zp(d):
        return dev(g, y, (c + d) % 8)

    def yp(d):
        return dev(g, (y + d) % 8, c)

    def go(e):
        return 2 * ((x + e[0]) % 4) + (q + e[1]) % 2

    def gp(e):
        return dev(go(e), y, c)

    sent = []

    def send(src, dst, ssem, rsem, to):
        cp = pltpu.make_async_remote_copy(
            src_ref=src, dst_ref=dst, send_sem=ssem, recv_sem=rsem, device_id=to, device_id_type=MESH
        )
        cp.start()
        sent.append(cp)

    def arrived(dst, rsem):
        pltpu.make_async_remote_copy(
            src_ref=dst, dst_ref=dst, send_sem=rsem, recv_sem=rsem, device_id=zp(1), device_id_type=MESH
        ).wait_recv()

    turned = dev(c, y, g)
    moves = g != c
    barrier = pltpu.get_barrier_semaphore()
    for d in NEAR:
        pl.semaphore_signal(barrier, inc=1, device_id=zp(d), device_id_type=MESH)
        pl.semaphore_signal(barrier, inc=1, device_id=yp(d), device_id_type=MESH)
    for e in GROUP:
        pl.semaphore_signal(barrier, inc=1, device_id=gp(e), device_id_type=MESH)

    @pl.when(moves)
    def _():
        pl.semaphore_signal(barrier, inc=1, device_id=turned, device_id_type=MESH)

    pl.semaphore_wait(barrier, 21 + jnp.where(moves, 1, 0))

    for d in FAR:
        send(rhs.at[0], rz.at[c], s_rz.at[d], q_rz.at[c], zp(d))
    for i, e in enumerate(GROUP):
        send(inv.at[0], m0.at[g], s_m.at[0, i], q_m.at[0, g], gp(e))
    turn = pltpu.make_async_remote_copy(
        src_ref=rhs.at[1], dst_ref=r1t, send_sem=s_r1.at[0], recv_sem=q_r1.at[0], device_id=turned, device_id_type=MESH
    )

    @pl.when(moves)
    def _():
        turn.start()

    @pl.when(jnp.logical_not(moves))
    def _():
        r1t[...] = rhs[1]

    m0[g] = inv[0]
    m1[g] = pan1[0]
    m2[g] = inv[1]
    rz[c] = rhs[0]

    for i, e in enumerate(GROUP):
        to = go(e)

        @pl.when(to != c)
        def _():
            arrived(rz.at[to], q_rz.at[to])

        send(rz.at[to], r.at[g], s_r.at[i], q_r.at[g], gp(e))

    @pl.when(g != c)
    def _():
        arrived(rz.at[g], q_rz.at[g])

    r[g] = rz[g]
    for i, e in enumerate(GROUP):
        send(pan1.at[0], m1.at[g], s_m.at[1, i], q_m.at[1, g], gp(e))
    for i, e in enumerate(GROUP):
        send(inv.at[1], m2.at[g], s_m.at[2, i], q_m.at[2, g], gp(e))

    def split_panel(pan, first, hi, lo):
        h, l = split(pan[first:first + 14].reshape(448, 256))
        hi[...] = h
        lo[...] = l

    split_panel(pan2, 0, p2h, p2l)

    for e in GROUP:
        arrived(m0.at[go(e)], q_m.at[0, go(e)])
    m0s = split(m0[...].reshape(256, 256).T)
    for e in GROUP:
        arrived(r.at[go(e)], q_r.at[go(e)])

    def reduce_start(out, part, inn, ss, qs, peer, me):
        out[...] = part.reshape(8, 32, 128)
        for d in FAR:
            send(out.at[(me + d) % 8], inn.at[d], ss.at[d], qs.at[d], peer(d))

    def reduce_end(out, inn, qs, me):
        total = out[me]
        for d in NEAR:
            arrived(inn.at[d], qs.at[d])
            total = total + inn[d]
        return total

    reduce_start(pa, dot3(m0s, split(r[...].reshape(256, 128))), pa_in, s_a, q_a, yp, y)
    split_panel(pan1, 1, p1h, p1l)
    full[0, g, y] = reduce_end(pa, pa_in, q_a, y)
    for d in FAR:
        send(full.at[0, g, y], full.at[0, g, y], s_f.at[d], q_f.at[y], yp(d))
    for e in GROUP:
        arrived(m1.at[go(e)], q_m.at[1, go(e)])
    m1s = split(m1[...].reshape(256, 256))
    for d in NEAR:
        arrived(full.at[0, g, (y + d) % 8], q_f.at[(y + d) % 8])

    reduce_start(pb, dot3(m1s, split(full[0, g].reshape(256, 128))), pb_in, s_b, q_b, zp, c)
    for i in (2, 1, 3):
        send(full.at[0, g], full.at[0, g], s_fx.at[i], q_fx.at[i], gp((i, 0)))
    send(full.at[0, g], full.at[0, g], s_fc.at[0], q_fc.at[0], gp((0, 1)))
    for e in GROUP:
        arrived(m2.at[go(e)], q_m.at[2, go(e)])
    m2s = split(m2[...].reshape(256, 256).T)

    @pl.when(moves)
    def _():
        turn.wait()

    u[c] = r1t[...] - reduce_end(pb, pb_in, q_b, c)
    for d in FAR:
        send(u.at[c], u.at[c], s_u.at[d], q_u.at[c], zp(d))
    for i in (1, 3, 2):
        came = go((4 - i, 0))
        arrived(full.at[0, came], q_fx.at[i])
        send(full.at[0, came], full.at[0, came], s_fc.at[i], q_fc.at[i], gp((0, 1)))
    for d in NEAR:
        arrived(u.at[(c + d) % 8], q_u.at[(c + d) % 8])

    reduce_start(pc, dot3(m2s, split(u[...].reshape(256, 128))), pc_in, s_c, q_c, yp, y)
    for i in range(4):
        arrived(full.at[0, go(((4 - i) % 4, 1))], q_fc.at[i])

    def first_products(j, carry):
        b = jnp.concatenate([full[0, 2 * j].reshape(256, 128), full[0, 2 * j + 1].reshape(256, 128)], axis=1)
        o = dot3((p1h[...], p1l[...]), split(b))
        acc[2 * j] = o[:, :128].reshape(14, 32, 128)
        acc[2 * j + 1] = o[:, 128:].reshape(14, 32, 128)
        return carry

    lax.fori_loop(0, 4, first_products, 0)
    full[1, g, y] = reduce_end(pc, pc_in, q_c, y)

    def pass_on(k, yy):
        for i in (2, 1, 3):
            send(full.at[1, g, yy], full.at[1, g, yy], s_sx.at[i, k], q_sx.at[i, k], gp((i, 0)))
        send(full.at[1, g, yy], full.at[1, g, yy], s_sc.at[0, k], q_sc.at[0, k], gp((0, 1)))

    for d in FAR:
        send(full.at[1, g, y], full.at[1, g, y], s_s.at[d], q_s.at[y], yp(d))
    pass_on(0, y)
    for d in NEAR:
        yy = (y + d) % 8
        arrived(full.at[1, g, yy], q_s.at[yy])
        pass_on(d, yy)
    for d in (0, *NEAR):
        yy = (y + d) % 8
        for i in (1, 3, 2):
            came = go((4 - i, 0))
            arrived(full.at[1, came, yy], q_sx.at[i, d])
            send(full.at[1, came, yy], full.at[1, came, yy], s_sc.at[i, d], q_sc.at[i, d], gp((0, 1)))
    for d in (0, *NEAR):
        yy = (y + d) % 8
        for i in range(4):
            arrived(full.at[1, go(((4 - i) % 4, 1)), yy], q_sc.at[i, d])

    def second_products(k):
        b = split(full[1, k].reshape(256, 128))
        acc[k] += dot3((p2h[...], p2l[...]), b).reshape(14, 32, 128)

    ways = ((1, 0, 0), (-1, 1, 1))

    def at(s, n):
        return (c + s * n + 8) % 8

    def half(h):
        return pl.ds(7 * h, 7)

    def hop1(s, w, h, t):
        k = at(s, 4 - t)
        if t == 0:
            src = acc.at[k, half(h)]
        else:
            src = ring1.at[w, t - 1]
            arrived(src, q_1.at[w, t - 1])
            src[...] += acc[k, half(h)]
        send(src, ring1.at[w, t], s_1.at[w, t], q_1.at[w, t], zp(s + 8))

    def hop2(s, w, h, t):
        k = at(s, 3 - t)
        if t == 0:
            src = acc.at[k, half(1 - h)]
        else:
            src = ring2.at[w, t - 1]
            arrived(src, q_2.at[w, t - 1])
            src[...] += acc[k, half(1 - h)]
        send(src, ring2.at[w, t], s_2.at[w, t], q_2.at[w, t], zp(s + 8))

    second_products(at(1, 4))
    for s, w, h in ways:
        hop1(s, w, h, 0)
    for s, w, h in ways:
        second_products(at(s, 3))
        hop2(s, w, h, 0)
    for s, w, h in ways:
        hop1(s, w, h, 1)
    for s, w, h in ways:
        second_products(at(s, 2))
        hop2(s, w, h, 1)
    for s, w, h in ways:
        hop1(s, w, h, 2)
    for s, w, h in ways:
        second_products(at(s, 1))
        hop2(s, w, h, 2)
    for s, w, h in ways:
        hop1(s, w, h, 3)
    second_products(c)
    for i in range(2):
        for k in range(8):
            sol[i, :, 128 * k:128 * (k + 1)] = full[i, k].reshape(256, 128)
    rem[...] = rhs[2:] - acc[c]
    for s, w, h in ways:
        arrived(ring2.at[w, 2], q_2.at[w, 2])
        rem[half(1 - h)] -= ring2[w, 2]
    for s, w, h in ways:
        arrived(ring1.at[w, 3], q_1.at[w, 3])
        rem[half(h)] -= ring1[w, 3]
    for cp in sent:
        cp.wait_send()


def shards(right_sides, first_panel, second_panel, inverse_transposed):
    vmem = pl.BlockSpec(memory_space=pltpu.VMEM)

    def block(*shape):
        return pltpu.VMEM(shape, F32)

    def dma(*shape):
        return pltpu.SemaphoreType.DMA(shape)

    piece, matrix = (8, 32, 128), (8, 32, 256)
    return pl.pallas_call(
        kernel,
        out_shape=(
            jax.ShapeDtypeStruct((2, 256, 1024), F32),
            jax.ShapeDtypeStruct((14, 32, 128), F32),
        ),
        in_specs=[vmem] * 4,
        out_specs=(vmem, vmem),
        scratch_shapes=[
            block(*piece), block(*piece), block(*matrix), block(*matrix), block(*matrix), block(32, 128),
            block(*piece), block(*piece), block(*piece), block(*piece), block(*piece), block(*piece), block(*piece),
            block(2, 8, 8, 32, 128), block(8, 14, 32, 128),
            pltpu.VMEM((448, 256), BF16), pltpu.VMEM((448, 256), BF16),
            pltpu.VMEM((448, 256), BF16), pltpu.VMEM((448, 256), BF16),
            block(2, 4, 7, 32, 128), block(2, 3, 7, 32, 128),
            dma(8), dma(8), dma(3, 7), dma(3, 8), dma(1), dma(1), dma(7), dma(8), dma(8), dma(8),
            dma(8), dma(8), dma(4), dma(4), dma(4), dma(4),
            dma(8), dma(8), dma(8), dma(8), dma(8), dma(8), dma(8), dma(8),
            dma(4, 8), dma(4, 8), dma(4, 8), dma(4, 8), dma(2, 4), dma(2, 4), dma(2, 3), dma(2, 3),
        ],
        compiler_params=pltpu.CompilerParams(
            collective_id=0, has_side_effects=True, vmem_limit_bytes=48 * 1024 * 1024
        ),
        cost_estimate=pl.CostEstimate(flops=1500000000, bytes_accessed=5000000, transcendentals=0),
    )(right_sides, first_panel, second_panel, inverse_transposed)


def solution(mesh):
    return jax.shard_map(
        shards,
        mesh=mesh,
        in_specs=(
            P(None, "row", "col"),
            P(None, "row", "col"),
            P(None, "row", "col"),
            P(None, "row", "col"),
        ),
        out_specs=(P(None, "col", None), P(None, "row", "col")),
        check_vma=False,
    )
```

```python
import functools

import jax
import jax.numpy as jnp
from jax import lax
from jax.experimental import pallas as pl
from jax.experimental.pallas import tpu as pltpu
from jax.sharding import PartitionSpec as P

MESH = pl.DeviceIdType.MESH
F32 = jnp.float32
BF16 = jnp.bfloat16

NEAR = (1, 7, 2, 6, 3, 5, 4)
FAR = NEAR[::-1]
SLOT = (0, 1, 3, 5, 7, 6, 4, 2)
PARTS = ((0, 1), (1, 3), (3, 5), (5, 8))
GROUP = ((2, 0), (2, 1), (1, 0), (3, 0), (1, 1), (3, 1), (0, 1))


def split(a):
    hi = a.astype(BF16)
    return hi, (a - hi.astype(F32)).astype(BF16)


def dot(a, b):
    return jnp.dot(a, b, preferred_element_type=F32)


def dot3(a, b):
    (ah, al), (bh, bl) = a, b
    return dot(ah, bh) + (dot(al, bh) + dot(ah, bl))


def kernel(
    rhs_h, pan1_h, pan2_h, inv_h, sol, rem,
    rhs, pan1, pan2, s_in, r, m0, m1, m2, r1t, pa, pa_in, pb, pb_in, u, pc, pc_in,
    full, acc, p1h, p1l, p2h, p2l, ring1, ring2,
    s_m, q_m, s_r1, q_r1, s_r, q_r, s_a, q_a, s_f, q_f, s_fx, q_fx, s_fc, q_fc,
    s_b, q_b, s_u, q_u, s_c, q_c, s_s, q_s, s_sx, q_sx, s_sc, q_sc, s_1, q_1, s_2, q_2,
):
    row = lax.axis_index("row")
    c = lax.axis_index("col")
    x, y, q = row // 16, (row // 2) % 8, row % 2
    g = 2 * x + q

    def dev(gg, yy, cc):
        return (((gg // 2) * 8 + yy) * 2 + gg % 2, cc)

    def zp(d):
        return dev(g, y, (c + d) % 8)

    def yp(d):
        return dev(g, (y + d) % 8, c)

    def go(e):
        return 2 * ((x + e[0]) % 4) + (q + e[1]) % 2

    def gp(e):
        return dev(go(e), y, c)

    sent = []

    def send(src, dst, ssem, rsem, to, when=None):
        cp = pltpu.make_async_remote_copy(
            src_ref=src, dst_ref=dst, send_sem=ssem, recv_sem=rsem, device_id=to, device_id_type=MESH
        )
        if when is None:
            cp.start()
        else:
            pl.when(when)(cp.start)
        sent.append((when, cp))

    def arrived(dst, rsem):
        pltpu.make_async_remote_copy(
            src_ref=dst, dst_ref=dst, send_sem=rsem, recv_sem=rsem, device_id=zp(1), device_id_type=MESH
        ).wait_recv()

    loads = [
        pltpu.make_async_copy(src, dst, s_in.at[i])
        for i, (src, dst) in enumerate((
            (rhs_h, rhs), (inv_h.at[0], m0.at[g]), (pan1_h.at[0], m1.at[g]), (inv_h.at[1], m2.at[g]),
            (pan2_h, pan2), (pan1_h.at[pl.ds(1, 14)], pan1),
        ))
    ]
    for load in loads:
        load.start()

    turned = dev(c, y, g)
    moves = g != c
    barrier = pltpu.get_barrier_semaphore()
    for d in NEAR:
        pl.semaphore_signal(barrier, inc=1, device_id=zp(d), device_id_type=MESH)
        pl.semaphore_signal(barrier, inc=1, device_id=yp(d), device_id_type=MESH)
    for e in GROUP:
        pl.semaphore_signal(barrier, inc=1, device_id=gp(e), device_id_type=MESH)
    for e in GROUP:
        pl.semaphore_signal(barrier, inc=1, device_id=dev(go(e), y, g), device_id_type=MESH)

    @pl.when(moves)
    def _():
        pl.semaphore_signal(barrier, inc=1, device_id=dev(g, y, g), device_id_type=MESH)

    for load in loads[:4]:
        load.wait()
    pl.semaphore_wait(barrier, 28 + jnp.where(moves, 1, 0))

    for d in FAR:
        send(rhs.at[0], r.at[g], s_r.at[d], q_r.at[g], dev(c, y, (c + d) % 8))
    here = pltpu.make_async_remote_copy(
        src_ref=rhs.at[0], dst_ref=r.at[g], send_sem=s_r.at[0], recv_sem=q_r.at[g],
        device_id=dev(c, y, c), device_id_type=MESH,
    )
    turn = pltpu.make_async_remote_copy(
        src_ref=rhs.at[1], dst_ref=r1t, send_sem=s_r1.at[0], recv_sem=q_r1.at[0], device_id=turned, device_id_type=MESH
    )

    @pl.when(moves)
    def _():
        here.start()

    @pl.when(jnp.logical_not(moves))
    def _():
        r[g] = rhs[0]
        r1t[...] = rhs[1]

    for i, e in enumerate(GROUP):
        send(m0.at[g], m0.at[g], s_m.at[0, i], q_m.at[0, g], gp(e))

    @pl.when(moves)
    def _():
        turn.start()

    for i, e in enumerate(GROUP):
        send(m1.at[g], m1.at[g], s_m.at[1, i], q_m.at[1, g], gp(e))
    for i, e in enumerate(GROUP):
        send(m2.at[g], m2.at[g], s_m.at[2, i], q_m.at[2, g], gp(e))

    def split_panel(pan, hi, lo):
        h, l = split(pan[...].reshape(448, 256))
        hi[...] = h
        lo[...] = l

    for load in loads[4:]:
        load.wait()
    split_panel(pan2, p2h, p2l)

    for e in GROUP:
        arrived(m0.at[go(e)], q_m.at[0, go(e)])
    m0s = split(m0[...].reshape(256, 256).T)
    for e in GROUP:
        arrived(r.at[go(e)], q_r.at[go(e)])

    @pl.when(moves)
    def _():
        arrived(r.at[g], q_r.at[g])

    def whole(i, k):
        d = [(n - y + 8) % 8 for n in range(8)]
        at = [jnp.where(n == 0, 0, jnp.where(n <= 4, 2 * n - 1, 16 - 2 * n)) for n in d]
        return jnp.concatenate([full[i, k, n] for n in at], axis=0)

    def reduce_start(out, part, inn, ss, qs, peer, me):
        out[...] = part.reshape(8, 32, 128)
        for d in FAR:
            send(out.at[(me + d) % 8], inn.at[d], ss.at[d], qs.at[d], peer(d))

    def reduce_end(out, inn, qs, me):
        total = out[me]
        for d in NEAR:
            arrived(inn.at[d], qs.at[d])
            total = total + inn[d]
        return total

    reduce_start(pa, dot3(m0s, split(r[...].reshape(256, 128))), pa_in, s_a, q_a, yp, y)
    split_panel(pan1, p1h, p1l)
    full[0, g, 0] = reduce_end(pa, pa_in, q_a, y)
    for d in FAR:
        send(full.at[0, g, 0], full.at[0, g, SLOT[8 - d]], s_f.at[d], q_f.at[8 - d], yp(d))
    for e in GROUP:
        arrived(m1.at[go(e)], q_m.at[1, go(e)])
    m1s = split(m1[...].reshape(256, 256))
    for d in NEAR:
        arrived(full.at[0, g, SLOT[d]], q_f.at[d])

    reduce_start(pb, dot3(m1s, split(whole(0, g))), pb_in, s_b, q_b, zp, c)
    for i in (2, 1, 3):
        send(full.at[0, g], full.at[0, g], s_fx.at[i], q_fx.at[i], gp((i, 0)))
    send(full.at[0, g], full.at[0, g], s_fc.at[0], q_fc.at[0], gp((0, 1)))
    for e in GROUP:
        arrived(m2.at[go(e)], q_m.at[2, go(e)])
    m2s = split(m2[...].reshape(256, 256).T)

    @pl.when(moves)
    def _():
        turn.wait()

    u[c] = r1t[...] - reduce_end(pb, pb_in, q_b, c)
    for d in FAR:
        send(u.at[c], u.at[c], s_u.at[d], q_u.at[c], zp(d))
    for i in (1, 3, 2):
        came = go((4 - i, 0))
        arrived(full.at[0, came], q_fx.at[i])
        send(full.at[0, came], full.at[0, came], s_fc.at[i], q_fc.at[i], gp((0, 1)))
    for d in NEAR:
        arrived(u.at[(c + d) % 8], q_u.at[(c + d) % 8])

    reduce_start(pc, dot3(m2s, split(u[...].reshape(256, 128))), pc_in, s_c, q_c, yp, y)
    for i in range(4):
        arrived(full.at[0, go(((4 - i) % 4, 1))], q_fc.at[i])

    def first_products(j, carry):
        b = jnp.concatenate([whole(0, 2 * j), whole(0, 2 * j + 1)], axis=1)
        o = dot3((p1h[...], p1l[...]), split(b))
        acc[2 * j] = o[:, :128].reshape(14, 32, 128)
        acc[2 * j + 1] = o[:, 128:].reshape(14, 32, 128)
        return carry

    lax.fori_loop(0, 4, first_products, 0)
    full[1, g, 0] = reduce_end(pc, pc_in, q_c, y)

    def soon(k):
        return (jnp.abs((k - c + 8) % 8 - 4) <= 1)

    def parts(k, n):
        lo, hi = PARTS[n] if n < 4 else (0, 8)
        return full.at[1, k, pl.ds(lo, hi - lo)]

    def pass_on(n, when):
        part = parts(g, n)
        for i in (2, 1, 3):
            send(part, part, s_sx.at[i, n], q_sx.at[i, n], gp((i, 0)), when)
        send(part, part, s_sc.at[0, n], q_sc.at[0, n], gp((0, 1)), when)

    def forward(n, when, done=False):
        for i in (1, 3, 2):
            k = go((4 - i, 0))
            part = parts(k, n)
            cp = pltpu.make_async_remote_copy(
                src_ref=part, dst_ref=part, send_sem=s_sc.at[i, n], recv_sem=q_sc.at[i, n],
                device_id=gp((0, 1)), device_id_type=MESH,
            )

            @pl.when(when(k))
            def _():
                if done:
                    cp.wait_send()
                else:
                    arrived(part, q_sx.at[i, n])
                    cp.start()

    def late(k):
        return jnp.logical_not(soon(k))

    for d in FAR:
        send(full.at[1, g, 0], full.at[1, g, SLOT[8 - d]], s_s.at[d], q_s.at[8 - d], yp(d))
    for n, (lo, hi) in enumerate(PARTS):
        for d in range(1, 8):
            if lo <= SLOT[d] < hi:
                arrived(full.at[1, g, SLOT[d]], q_s.at[d])
        pass_on(n, soon(g))
    pass_on(4, late(g))
    for n in range(4):
        forward(n, soon)

    def second_products(k):
        other = k % 2 != q
        i = (x - k // 2 + 4) % 4

        @pl.when(jnp.logical_and(other, soon(k)))
        def _():
            for n in range(4):
                arrived(parts(k, n), q_sc.at[i, n])

        @pl.when(jnp.logical_and(other, late(k)))
        def _():
            arrived(parts(k, 4), q_sc.at[i, 4])

        acc[k] += dot3((p2h[...], p2l[...]), split(whole(1, k))).reshape(14, 32, 128)

    ways = ((1, 0, 0), (-1, 1, 1))

    def half(h):
        return pl.ds(7 * h, 7)

    def hop(ring, hops, ss, qs, s, w, h, t):
        k = (c + s * (hops - t) + 8) % 8
        out = ring.at[w, t]

        @pl.when(t == 0)
        def _():
            out[...] = acc[k, half(h)]

        @pl.when(t > 0)
        def _():
            arrived(out, qs.at[w, t])
            out[...] += acc[k, half(h)]

        pltpu.make_async_remote_copy(
            src_ref=out, dst_ref=ring.at[w, t + 1], send_sem=ss.at[w, t], recv_sem=qs.at[w, t + 1],
            device_id=zp(s + 8), device_id_type=MESH,
        ).start()

    def hop1(s, w, h, t):
        hop(ring1, 4, s_1, q_1, s, w, h, t)

    def hop2(s, w, h, t):
        hop(ring2, 3, s_2, q_2, s, w, 1 - h, t)

    def step(n, carry):
        second_products((c + jnp.where(n % 2 == 1, 4 - (n + 1) // 2, 4 + n // 2)) % 8)

        @pl.when(n == 0)
        def _():
            for s, w, h in ways:
                hop1(s, w, h, 0)

        @pl.when(jnp.logical_and(n % 2 == 1, n < 7))
        def _():
            hop2(*ways[0], (n - 1) // 2)

        @pl.when(jnp.logical_and(n % 2 == 0, n > 0))
        def _():
            hop2(*ways[1], (n - 2) // 2)

        @pl.when(n == 2)
        def _():
            forward(4, late)

        @pl.when(jnp.logical_and(n % 2 == 0, n > 0))
        def _():
            for s, w, h in ways:
                hop1(s, w, h, n // 2)

        return carry

    lax.fori_loop(0, 8, step, 0)
    for i in range(2):
        for k in range(8):
            sol[i, :, 128 * k:128 * (k + 1)] = whole(i, k)
    rem[...] = rhs[2:] - acc[c]
    for s, w, h in ways:
        arrived(ring2.at[w, 3], q_2.at[w, 3])
        rem[half(1 - h)] -= ring2[w, 3]
    for s, w, h in ways:
        arrived(ring1.at[w, 4], q_1.at[w, 4])
        rem[half(h)] -= ring1[w, 4]
    for when, cp in sent:
        if when is None:
            cp.wait_send()
        else:
            pl.when(when)(cp.wait_send)
    for n in range(5):
        forward(n, soon if n < 4 else late, True)
    for ring, hops, ss in ((ring1, 4, s_1), (ring2, 3, s_2)):
        for w in range(2):
            for t in range(hops):
                pltpu.make_async_remote_copy(
                    src_ref=ring.at[w, t], dst_ref=ring.at[w, t], send_sem=ss.at[w, t], recv_sem=ss.at[w, t],
                    device_id=zp(1), device_id_type=MESH,
                ).wait_send()

    @pl.when(moves)
    def _():
        here.wait_send()


def shards(*args):
    vmem = pl.BlockSpec(memory_space=pltpu.VMEM)
    outside = pl.BlockSpec(memory_space=pltpu.HBM)

    def block(*shape):
        return pltpu.VMEM(shape, F32)

    def dma(*shape):
        return pltpu.SemaphoreType.DMA(shape)

    piece, matrix = (8, 32, 128), (8, 32, 256)
    return pl.pallas_call(
        kernel,
        out_shape=(
            jax.ShapeDtypeStruct((2, 256, 1024), F32),
            jax.ShapeDtypeStruct((14, 32, 128), F32),
        ),
        in_specs=[outside] * 4,
        out_specs=(vmem, vmem),
        scratch_shapes=[
            block(16, 32, 128), block(14, 32, 256), block(14, 32, 256), dma(6),
            block(*piece), block(*matrix), block(*matrix), block(*matrix), block(32, 128),
            block(*piece), block(*piece), block(*piece), block(*piece), block(*piece), block(*piece), block(*piece),
            block(2, 8, 8, 32, 128), block(8, 14, 32, 128),
            pltpu.VMEM((448, 256), BF16), pltpu.VMEM((448, 256), BF16),
            pltpu.VMEM((448, 256), BF16), pltpu.VMEM((448, 256), BF16),
            block(2, 5, 7, 32, 128), block(2, 4, 7, 32, 128),
            dma(3, 7), dma(3, 8), dma(1), dma(1), dma(8), dma(8), dma(8), dma(8),
            dma(8), dma(8), dma(4), dma(4), dma(4), dma(4),
            dma(8), dma(8), dma(8), dma(8), dma(8), dma(8), dma(8), dma(8),
            dma(4, 5), dma(4, 5), dma(4, 5), dma(4, 5), dma(2, 5), dma(2, 5), dma(2, 4), dma(2, 4),
        ],
        compiler_params=pltpu.CompilerParams(
            collective_id=0, has_side_effects=True, vmem_limit_bytes=32 * 1024 * 1024
        ),
        cost_estimate=pl.CostEstimate(flops=1500000000, bytes_accessed=5000000, transcendentals=0),
    )(*(pltpu.with_memory_space_constraint(v, pltpu.HBM) for v in args))


def solution(mesh):
    return jax.shard_map(
        shards,
        mesh=mesh,
        in_specs=(
            P(None, "row", "col"),
            P(None, "row", "col"),
            P(None, "row", "col"),
            P(None, "row", "col"),
        ),
        out_specs=(P(None, "col", None), P(None, "row", "col")),
        check_vma=False,
    )
```

```python
import functools

import jax
import jax.numpy as jnp
from jax import lax
from jax.experimental import pallas as pl
from jax.experimental.pallas import tpu as pltpu
from jax.sharding import PartitionSpec as P

MESH = pl.DeviceIdType.MESH
F32 = jnp.float32
BF16 = jnp.bfloat16

NEAR = (1, 7, 2, 6, 3, 5, 4)
FAR = NEAR[::-1]
SLOT = (0, 1, 3, 5, 7, 6, 4, 2)
PARTS = ((0, 3), (3, 8))
PIECES = ((0, 4), (4, 7))
GROUP = ((2, 0), (2, 1), (1, 0), (3, 0), (1, 1), (3, 1), (0, 1))


def split(a):
    hi = a.astype(BF16)
    return hi, (a - hi.astype(F32)).astype(BF16)


def dot(a, b):
    return jnp.dot(a, b, preferred_element_type=F32)


def dot3(a, b):
    (ah, al), (bh, bl) = a, b
    return dot(ah, bh) + (dot(al, bh) + dot(ah, bl))


def kernel(
    rhs_h, pan1_h, pan2_h, inv_h, sol, rem,
    rhs, pan1, pan2, s_in, r, m0, m1, m2, r1t, pa, pa_in, pb, pb_in, u, pc, pc_in,
    full, acc, p1h, p1l, p2h, p2l, ring1, ring2,
    s_m, q_m, s_r1, q_r1, s_r, q_r, s_a, q_a, s_f, q_f, s_fx, q_fx, s_fc, q_fc,
    s_b, q_b, s_u, q_u, s_c, q_c, s_s, q_s, s_t, q_t, s_sx, q_sx, s_sc, q_sc, s_1, q_1, s_2, q_2,
):
    row = lax.axis_index("row")
    c = lax.axis_index("col")
    x, y, q = row // 16, (row // 2) % 8, row % 2
    g = 2 * x + q

    def dev(gg, yy, cc):
        return (((gg // 2) * 8 + yy) * 2 + gg % 2, cc)

    def zp(d):
        return dev(g, y, (c + d) % 8)

    def yp(d):
        return dev(g, (y + d) % 8, c)

    def go(e):
        return 2 * ((x + e[0]) % 4) + (q + e[1]) % 2

    def gp(e):
        return dev(go(e), y, c)

    sent = []

    def send(src, dst, ssem, rsem, to, when=None):
        cp = pltpu.make_async_remote_copy(
            src_ref=src, dst_ref=dst, send_sem=ssem, recv_sem=rsem, device_id=to, device_id_type=MESH
        )
        if when is None:
            cp.start()
        else:
            pl.when(when)(cp.start)
        sent.append((when, cp))

    def arrived(dst, rsem):
        pltpu.make_async_remote_copy(
            src_ref=dst, dst_ref=dst, send_sem=rsem, recv_sem=rsem, device_id=zp(1), device_id_type=MESH
        ).wait_recv()

    loads = [
        pltpu.make_async_copy(src, dst, s_in.at[i])
        for i, (src, dst) in enumerate((
            (rhs_h, rhs), (inv_h.at[0], m0.at[g]), (pan1_h.at[0], m1.at[g]), (inv_h.at[1], m2.at[g]),
            (pan2_h, pan2), (pan1_h.at[pl.ds(1, 14)], pan1),
        ))
    ]
    for load in loads:
        load.start()

    turned = dev(c, y, g)
    moves = g != c
    barrier = pltpu.get_barrier_semaphore()
    for d in NEAR:
        pl.semaphore_signal(barrier, inc=1, device_id=zp(d), device_id_type=MESH)
        pl.semaphore_signal(barrier, inc=1, device_id=yp(d), device_id_type=MESH)
    for e in GROUP:
        pl.semaphore_signal(barrier, inc=1, device_id=gp(e), device_id_type=MESH)
    for e in GROUP:
        pl.semaphore_signal(barrier, inc=1, device_id=dev(go(e), y, g), device_id_type=MESH)

    @pl.when(moves)
    def _():
        pl.semaphore_signal(barrier, inc=1, device_id=dev(g, y, g), device_id_type=MESH)

    for load in loads[:4]:
        load.wait()
    pl.semaphore_wait(barrier, 28 + jnp.where(moves, 1, 0))

    for d in FAR:
        send(rhs.at[0], r.at[g], s_r.at[d], q_r.at[g], dev(c, y, (c + d) % 8))
    here = pltpu.make_async_remote_copy(
        src_ref=rhs.at[0], dst_ref=r.at[g], send_sem=s_r.at[0], recv_sem=q_r.at[g],
        device_id=dev(c, y, c), device_id_type=MESH,
    )
    turn = pltpu.make_async_remote_copy(
        src_ref=rhs.at[1], dst_ref=r1t, send_sem=s_r1.at[0], recv_sem=q_r1.at[0], device_id=turned, device_id_type=MESH
    )

    @pl.when(moves)
    def _():
        here.start()

    @pl.when(jnp.logical_not(moves))
    def _():
        r[g] = rhs[0]
        r1t[...] = rhs[1]

    for i, e in enumerate(GROUP):
        send(m0.at[g], m0.at[g], s_m.at[0, i], q_m.at[0, g], gp(e))

    @pl.when(moves)
    def _():
        turn.start()

    for i, e in enumerate(GROUP):
        send(m1.at[g], m1.at[g], s_m.at[1, i], q_m.at[1, g], gp(e))
    for i, e in enumerate(GROUP):
        send(m2.at[g], m2.at[g], s_m.at[2, i], q_m.at[2, g], gp(e))

    def split_panel(pan, hi, lo):
        h, l = split(pan[...].reshape(448, 256))
        hi[...] = h
        lo[...] = l

    for load in loads[4:]:
        load.wait()
    split_panel(pan2, p2h, p2l)

    for e in GROUP:
        arrived(m0.at[go(e)], q_m.at[0, go(e)])
    m0s = split(m0[...].reshape(256, 256).T)
    for e in GROUP:
        arrived(r.at[go(e)], q_r.at[go(e)])

    @pl.when(moves)
    def _():
        arrived(r.at[g], q_r.at[g])

    def whole(i, k):
        d = [(n - y + 8) % 8 for n in range(8)]
        at = [jnp.where(n == 0, 0, jnp.where(n <= 4, 2 * n - 1, 16 - 2 * n)) for n in d]
        return jnp.concatenate([full[i, k, n] for n in at], axis=0)

    def reduce_start(out, part, inn, ss, qs, peer, me):
        out[...] = part.reshape(8, 32, 128)
        for d in FAR:
            send(out.at[(me + d) % 8], inn.at[d], ss.at[d], qs.at[d], peer(d))

    def reduce_end(out, inn, qs, me):
        total = out[me]
        for d in NEAR:
            arrived(inn.at[d], qs.at[d])
            total = total + inn[d]
        return total

    reduce_start(pa, dot3(m0s, split(r[...].reshape(256, 128))), pa_in, s_a, q_a, yp, y)
    split_panel(pan1, p1h, p1l)
    full[0, g, 0] = reduce_end(pa, pa_in, q_a, y)
    for d in FAR:
        send(full.at[0, g, 0], full.at[0, g, SLOT[8 - d]], s_f.at[d], q_f.at[8 - d], yp(d))
    for e in GROUP:
        arrived(m1.at[go(e)], q_m.at[1, go(e)])
    m1s = split(m1[...].reshape(256, 256))
    for d in NEAR:
        arrived(full.at[0, g, SLOT[d]], q_f.at[d])

    reduce_start(pb, dot3(m1s, split(whole(0, g))), pb_in, s_b, q_b, zp, c)
    for i in (2, 1, 3):
        send(full.at[0, g], full.at[0, g], s_fx.at[i], q_fx.at[i], gp((i, 0)))
    send(full.at[0, g], full.at[0, g], s_fc.at[0], q_fc.at[0], gp((0, 1)))
    for e in GROUP:
        arrived(m2.at[go(e)], q_m.at[2, go(e)])
    m2s = split(m2[...].reshape(256, 256).T)

    @pl.when(moves)
    def _():
        turn.wait()

    u[c] = r1t[...] - reduce_end(pb, pb_in, q_b, c)
    for d in FAR:
        send(u.at[c], u.at[c], s_u.at[d], q_u.at[c], zp(d))
    for i in (1, 3, 2):
        came = go((4 - i, 0))
        arrived(full.at[0, came], q_fx.at[i])
        send(full.at[0, came], full.at[0, came], s_fc.at[i], q_fc.at[i], gp((0, 1)))
    for d in NEAR:
        arrived(u.at[(c + d) % 8], q_u.at[(c + d) % 8])

    reduce_start(pc, dot3(m2s, split(u[...].reshape(256, 128))), pc_in, s_c, q_c, yp, y)
    for i in range(4):
        arrived(full.at[0, go(((4 - i) % 4, 1))], q_fc.at[i])

    def first_products(j, carry):
        b = jnp.concatenate([whole(0, 2 * j), whole(0, 2 * j + 1)], axis=1)
        o = dot3((p1h[...], p1l[...]), split(b))
        acc[2 * j] = o[:, :128].reshape(14, 32, 128)
        acc[2 * j + 1] = o[:, 128:].reshape(14, 32, 128)
        return carry

    lax.fori_loop(0, 4, first_products, 0)
    full[1, g, 0] = reduce_end(pc, pc_in, q_c, y)

    far = go((2, 0))

    def part(k, n):
        lo, hi = PARTS[n]
        return full.at[1, k, pl.ds(lo, hi - lo)]

    def over_y(k, ss, qs):
        for d in FAR:
            send(full.at[1, k, 0], full.at[1, k, SLOT[8 - d]], ss.at[d], qs.at[8 - d], yp(d))

    def gathered(k, qs, n):
        lo, hi = PARTS[n]
        for d in NEAR:
            if lo <= SLOT[d] < hi:
                arrived(full.at[1, k, SLOT[d]], qs.at[d])

    def to_core(i, k, n):
        send(part(k, n), part(k, n), s_sc.at[i, n], q_sc.at[i, n], gp((0, 1)))

    send(full.at[1, g, 0], full.at[1, g, 0], s_sx.at[2, 0], q_sx.at[2, 0], gp((2, 0)))
    over_y(g, s_s, q_s)
    arrived(full.at[1, far, 0], q_sx.at[2, 0])
    over_y(far, s_t, q_t)
    for n in range(2):
        gathered(g, q_s, n)
        for i in (1, 3):
            send(part(g, n), part(g, n), s_sx.at[i, n], q_sx.at[i, n], gp((i, 0)))
        to_core(0, g, n)
    for n in range(2):
        for i in (1, 3):
            k = go((4 - i, 0))
            arrived(part(k, n), q_sx.at[i, n])
            to_core(i, k, n)
        gathered(far, q_t, n)
        to_core(2, far, n)

    def second_products(k):
        @pl.when(k % 2 != q)
        def _():
            for n in range(2):
                arrived(part(k, n), q_sc.at[(x - k // 2 + 4) % 4, n])

        acc[k] += dot3((p2h[...], p2l[...]), split(whole(1, k))).reshape(14, 32, 128)

    ways = ((1, 0, 0), (-1, 1, 1))

    def hop(ring, hops, ss, qs, s, w, h, t):
        k = (c + s * (hops - t) + 8) % 8
        for j, (lo, hi) in enumerate(PIECES):
            here_in = ring.at[w, t, pl.ds(lo, hi - lo)]
            own = acc.at[k, pl.ds(7 * h + lo, hi - lo)]

            @pl.when(t == 0)
            def _():
                here_in[...] = own[...]

            @pl.when(t > 0)
            def _():
                arrived(here_in, qs.at[w, t, j])
                here_in[...] += own[...]

            pltpu.make_async_remote_copy(
                src_ref=here_in, dst_ref=ring.at[w, t + 1, pl.ds(lo, hi - lo)],
                send_sem=ss.at[w, t, j], recv_sem=qs.at[w, t + 1, j],
                device_id=zp(s + 8), device_id_type=MESH,
            ).start()

    def hop1(s, w, h, t):
        hop(ring1, 4, s_1, q_1, s, w, h, t)

    def hop2(s, w, h, t):
        hop(ring2, 3, s_2, q_2, s, w, 1 - h, t)

    def step(n, carry):
        second_products((c + jnp.where(n % 2 == 1, 4 - (n + 1) // 2, 4 + n // 2)) % 8)

        @pl.when(n == 0)
        def _():
            for s, w, h in ways:
                hop1(s, w, h, 0)

        @pl.when(jnp.logical_and(n % 2 == 1, n < 7))
        def _():
            hop2(*ways[0], (n - 1) // 2)

        @pl.when(jnp.logical_and(n % 2 == 0, n > 0))
        def _():
            hop2(*ways[1], (n - 2) // 2)

        @pl.when(jnp.logical_and(n % 2 == 0, n > 0))
        def _():
            for s, w, h in ways:
                hop1(s, w, h, n // 2)

        return carry

    lax.fori_loop(0, 8, step, 0)
    for i in range(2):
        for k in range(8):
            sol[i, :, 128 * k:128 * (k + 1)] = whole(i, k)
    rem[...] = rhs[2:] - acc[c]
    for ring, last, qs, other in ((ring2, 3, q_2, 1), (ring1, 4, q_1, 0)):
        for s, w, h in ways:
            for j, (lo, hi) in enumerate(PIECES):
                arrived(ring.at[w, last, pl.ds(lo, hi - lo)], qs.at[w, last, j])
                rem[pl.ds(7 * (h ^ other) + lo, hi - lo)] -= ring[w, last, lo:hi]
    for when, cp in sent:
        if when is None:
            cp.wait_send()
        else:
            pl.when(when)(cp.wait_send)
    for ring, hops, ss in ((ring1, 4, s_1), (ring2, 3, s_2)):
        for w in range(2):
            for t in range(hops):
                for j, (lo, hi) in enumerate(PIECES):
                    out = ring.at[w, t, pl.ds(lo, hi - lo)]
                    pltpu.make_async_remote_copy(
                        src_ref=out, dst_ref=out, send_sem=ss.at[w, t, j], recv_sem=ss.at[w, t, j],
                        device_id=zp(1), device_id_type=MESH,
                    ).wait_send()

    @pl.when(moves)
    def _():
        here.wait_send()


def store(sol, rem, sol_out, rem_out, sem):
    copies = [
        pltpu.make_async_copy(src, dst, sem.at[i])
        for i, (src, dst) in enumerate(((sol.at[0], sol_out.at[0]), (sol.at[1], sol_out.at[1]), (rem, rem_out)))
    ]
    for copy in copies:
        copy.start()
    for copy in copies:
        copy.wait()


def shards(*args):
    vmem = pl.BlockSpec(memory_space=pltpu.VMEM)
    outside = pl.BlockSpec(memory_space=pltpu.HBM)

    def block(*shape):
        return pltpu.VMEM(shape, F32)

    def dma(*shape):
        return pltpu.SemaphoreType.DMA(shape)

    piece, matrix = (8, 32, 128), (8, 32, 256)
    outs = pl.pallas_call(
        kernel,
        out_shape=(
            jax.ShapeDtypeStruct((2, 256, 1024), F32),
            jax.ShapeDtypeStruct((14, 32, 128), F32),
        ),
        in_specs=[outside] * 4,
        out_specs=(vmem, vmem),
        scratch_shapes=[
            block(16, 32, 128), block(14, 32, 256), block(14, 32, 256), dma(6),
            block(*piece), block(*matrix), block(*matrix), block(*matrix), block(32, 128),
            block(*piece), block(*piece), block(*piece), block(*piece), block(*piece), block(*piece), block(*piece),
            block(2, 8, 8, 32, 128), block(8, 14, 32, 128),
            pltpu.VMEM((448, 256), BF16), pltpu.VMEM((448, 256), BF16),
            pltpu.VMEM((448, 256), BF16), pltpu.VMEM((448, 256), BF16),
            block(2, 5, 7, 32, 128), block(2, 4, 7, 32, 128),
            dma(3, 7), dma(3, 8), dma(1), dma(1), dma(8), dma(8), dma(8), dma(8),
            dma(8), dma(8), dma(4), dma(4), dma(4), dma(4),
            dma(8), dma(8), dma(8), dma(8), dma(8), dma(8), dma(8), dma(8),
            dma(8), dma(8), dma(4, 2), dma(4, 2), dma(4, 2), dma(4, 2), dma(2, 5, 2), dma(2, 5, 2), dma(2, 4, 2), dma(2, 4, 2),
        ],
        compiler_params=pltpu.CompilerParams(
            collective_id=0, has_side_effects=True, vmem_limit_bytes=32 * 1024 * 1024
        ),
        cost_estimate=pl.CostEstimate(flops=1500000000, bytes_accessed=5000000, transcendentals=0),
    )(*(pltpu.with_memory_space_constraint(v, pltpu.HBM) for v in args))
    return pl.pallas_call(
        store,
        out_shape=(
            jax.ShapeDtypeStruct((2, 256, 1024), F32),
            jax.ShapeDtypeStruct((14, 32, 128), F32),
        ),
        in_specs=[vmem] * 2,
        out_specs=(pl.BlockSpec(memory_space=pl.ANY),) * 2,
        scratch_shapes=[dma(3)],
    )(*(pltpu.with_memory_space_constraint(v, pltpu.VMEM) for v in outs))


def solution(mesh):
    return jax.shard_map(
        shards,
        mesh=mesh,
        in_specs=(
            P(None, "row", "col"),
            P(None, "row", "col"),
            P(None, "row", "col"),
            P(None, "row", "col"),
        ),
        out_specs=(P(None, "col", None), P(None, "row", "col")),
        check_vma=False,
    )
```

```python
import functools

import jax
import jax.numpy as jnp
from jax import lax
from jax.experimental import pallas as pl
from jax.experimental.pallas import tpu as pltpu
from jax.sharding import PartitionSpec as P

MESH = pl.DeviceIdType.MESH
F32 = jnp.float32
BF16 = jnp.bfloat16

NEAR = (1, 7, 2, 6, 3, 5, 4)
FAR = NEAR[::-1]
SLOT = (0, 1, 3, 5, 7, 6, 4, 2)
PARTS = ((0, 3), (3, 8))
PIECES = ((0, 4), (4, 7))
GROUP = ((2, 0), (2, 1), (1, 0), (3, 0), (1, 1), (3, 1), (0, 1))


def split(a):
    hi = a.astype(BF16)
    return hi, (a - hi.astype(F32)).astype(BF16)


def dot(a, b):
    return jnp.dot(a, b, preferred_element_type=F32)


def dot3(a, b):
    (ah, al), (bh, bl) = a, b
    return dot(ah, bh) + (dot(al, bh) + dot(ah, bl))


def kernel(
    rhs_h, pan1_h, pan2_h, inv_h, sol, rem,
    rhs, pan1, pan2, s_in, r, m0, m1, m2, r1t, pa, pa_in, pb, pb_in, u, pc, pc_in,
    full, acc, p1h, p1l, p2h, p2l, ring1, ring2,
    s_m, q_m, s_r1, q_r1, s_r, q_r, s_a, q_a, s_f, q_f, s_fx, q_fx, s_fc, q_fc,
    s_b, q_b, s_u, q_u, s_c, q_c, s_s, q_s, s_t, q_t, s_sx, q_sx, s_sc, q_sc, s_1, q_1, s_2, q_2,
):
    row = lax.axis_index("row")
    c = lax.axis_index("col")
    x, y, q = row // 16, (row // 2) % 8, row % 2
    g = 2 * x + q

    def dev(gg, yy, cc):
        return (((gg // 2) * 8 + yy) * 2 + gg % 2, cc)

    def zp(d):
        return dev(g, y, (c + d) % 8)

    def yp(d):
        return dev(g, (y + d) % 8, c)

    def go(e):
        return 2 * ((x + e[0]) % 4) + (q + e[1]) % 2

    def gp(e):
        return dev(go(e), y, c)

    sent = []

    def send(src, dst, ssem, rsem, to, when=None):
        cp = pltpu.make_async_remote_copy(
            src_ref=src, dst_ref=dst, send_sem=ssem, recv_sem=rsem, device_id=to, device_id_type=MESH
        )
        if when is None:
            cp.start()
        else:
            pl.when(when)(cp.start)
        sent.append((when, cp))

    def arrived(dst, rsem):
        pltpu.make_async_remote_copy(
            src_ref=dst, dst_ref=dst, send_sem=rsem, recv_sem=rsem, device_id=zp(1), device_id_type=MESH
        ).wait_recv()

    loads = [
        pltpu.make_async_copy(src, dst, s_in.at[i])
        for i, (src, dst) in enumerate((
            (rhs_h, rhs), (inv_h.at[0], m0.at[g]), (pan1_h.at[0], m1.at[g]), (inv_h.at[1], m2.at[g]),
            (pan2_h, pan2), (pan1_h.at[pl.ds(1, 14)], pan1),
        ))
    ]
    for load in loads:
        load.start()

    turned = dev(c, y, g)
    moves = g != c
    barrier = pltpu.get_barrier_semaphore()
    for d in NEAR:
        pl.semaphore_signal(barrier, inc=1, device_id=zp(d), device_id_type=MESH)
        pl.semaphore_signal(barrier, inc=1, device_id=yp(d), device_id_type=MESH)
    for e in GROUP:
        pl.semaphore_signal(barrier, inc=1, device_id=gp(e), device_id_type=MESH)
    for e in GROUP:
        pl.semaphore_signal(barrier, inc=1, device_id=dev(go(e), y, g), device_id_type=MESH)

    @pl.when(moves)
    def _():
        pl.semaphore_signal(barrier, inc=1, device_id=dev(g, y, g), device_id_type=MESH)

    for load in loads[:4]:
        load.wait()
    pl.semaphore_wait(barrier, 28 + jnp.where(moves, 1, 0))

    def uses(block, plane):
        return 2 * (block // 2) + y // 4 <= plane

    for d in FAR:
        send(rhs.at[0], r.at[g], s_r.at[d], q_r.at[g], dev(c, y, (c + d) % 8), uses(g, (c + d) % 8))
    here = pltpu.make_async_remote_copy(
        src_ref=rhs.at[0], dst_ref=r.at[g], send_sem=s_r.at[0], recv_sem=q_r.at[g],
        device_id=dev(c, y, c), device_id_type=MESH,
    )
    turn = pltpu.make_async_remote_copy(
        src_ref=rhs.at[1], dst_ref=r1t, send_sem=s_r1.at[0], recv_sem=q_r1.at[0], device_id=turned, device_id_type=MESH
    )

    @pl.when(jnp.logical_and(moves, uses(g, c)))
    def _():
        here.start()

    @pl.when(jnp.logical_not(moves))
    def _():
        r[g] = rhs[0]
        r1t[...] = rhs[1]

    for i, e in enumerate(GROUP):
        send(m0.at[g], m0.at[g], s_m.at[0, i], q_m.at[0, g], gp(e), uses(g, c))

    @pl.when(moves)
    def _():
        turn.start()

    for i, e in enumerate(GROUP):
        send(m1.at[g], m1.at[g], s_m.at[1, i], q_m.at[1, g], gp(e))
    for i, e in enumerate(GROUP):
        send(m2.at[g], m2.at[g], s_m.at[2, i], q_m.at[2, g], gp(e), uses(g, c))

    def split_panel(pan, hi, lo):
        h, l = split(pan[...].reshape(448, 256))
        hi[...] = h
        lo[...] = l

    for load in loads[4:]:
        load.wait()
    split_panel(pan2, p2h, p2l)

    def arrived_or_zero(buf, n, sem, needed):
        @pl.when(needed)
        def _():
            arrived(buf.at[n], sem)

        @pl.when(jnp.logical_not(needed))
        def _():
            buf[n] = jnp.zeros(buf.shape[1:], F32)

    for e in GROUP:
        arrived_or_zero(m0, go(e), q_m.at[0, go(e)], uses(go(e), c))
    m0s = split(m0[...].reshape(256, 256).T)
    for e in GROUP:
        arrived_or_zero(r, go(e), q_r.at[go(e)], uses(go(e), c))

    @pl.when(moves)
    def _():
        arrived_or_zero(r, g, q_r.at[g], uses(g, c))

    def whole(i, k):
        d = [(n - y + 8) % 8 for n in range(8)]
        at = [jnp.where(n == 0, 0, jnp.where(n <= 4, 2 * n - 1, 16 - 2 * n)) for n in d]
        return jnp.concatenate([full[i, k, n] for n in at], axis=0)

    def reduce_start(out, part, inn, ss, qs, peer, me):
        out[...] = part.reshape(8, 32, 128)
        for d in FAR:
            send(out.at[(me + d) % 8], inn.at[d], ss.at[d], qs.at[d], peer(d))

    def reduce_end(out, inn, qs, me):
        total = out[me]
        for d in NEAR:
            arrived(inn.at[d], qs.at[d])
            total = total + inn[d]
        return total

    reduce_start(pa, dot3(m0s, split(r[...].reshape(256, 128))), pa_in, s_a, q_a, yp, y)
    split_panel(pan1, p1h, p1l)
    full[0, g, 0] = reduce_end(pa, pa_in, q_a, y)
    for d in FAR:
        send(full.at[0, g, 0], full.at[0, g, SLOT[8 - d]], s_f.at[d], q_f.at[8 - d], yp(d))
    for e in GROUP:
        arrived(m1.at[go(e)], q_m.at[1, go(e)])
    m1s = split(m1[...].reshape(256, 256))
    for d in NEAR:
        arrived(full.at[0, g, SLOT[d]], q_f.at[d])

    reduce_start(pb, dot3(m1s, split(whole(0, g))), pb_in, s_b, q_b, zp, c)
    for i in (2, 1, 3):
        send(full.at[0, g], full.at[0, g], s_fx.at[i], q_fx.at[i], gp((i, 0)))
    send(full.at[0, g], full.at[0, g], s_fc.at[0], q_fc.at[0], gp((0, 1)))
    for e in GROUP:
        arrived_or_zero(m2, go(e), q_m.at[2, go(e)], uses(go(e), c))
    m2s = split(m2[...].reshape(256, 256).T)

    @pl.when(moves)
    def _():
        turn.wait()

    u[c] = r1t[...] - reduce_end(pb, pb_in, q_b, c)
    for d in FAR:
        send(u.at[c], u.at[c], s_u.at[d], q_u.at[c], zp(d), uses(c, (c + d) % 8))
    for i in (1, 3, 2):
        came = go((4 - i, 0))
        arrived(full.at[0, came], q_fx.at[i])
        send(full.at[0, came], full.at[0, came], s_fc.at[i], q_fc.at[i], gp((0, 1)))
    for d in NEAR:
        n = (c + d) % 8
        arrived_or_zero(u, n, q_u.at[n], uses(n, c))

    reduce_start(pc, dot3(m2s, split(u[...].reshape(256, 128))), pc_in, s_c, q_c, yp, y)
    for i in range(4):
        arrived(full.at[0, go(((4 - i) % 4, 1))], q_fc.at[i])

    def first_products(j, carry):
        b = jnp.concatenate([whole(0, 2 * j), whole(0, 2 * j + 1)], axis=1)
        o = dot3((p1h[...], p1l[...]), split(b))
        acc[2 * j] = o[:, :128].reshape(14, 32, 128)
        acc[2 * j + 1] = o[:, 128:].reshape(14, 32, 128)
        return carry

    lax.fori_loop(0, 4, first_products, 0)
    full[1, g, 0] = reduce_end(pc, pc_in, q_c, y)

    far = go((2, 0))

    def part(k, n):
        lo, hi = PARTS[n]
        return full.at[1, k, pl.ds(lo, hi - lo)]

    def over_y(k, ss, qs):
        for d in FAR:
            send(full.at[1, k, 0], full.at[1, k, SLOT[8 - d]], ss.at[d], qs.at[8 - d], yp(d))

    def gathered(k, qs, n):
        lo, hi = PARTS[n]
        for d in NEAR:
            if lo <= SLOT[d] < hi:
                arrived(full.at[1, k, SLOT[d]], qs.at[d])

    def to_core(i, k, n):
        send(part(k, n), part(k, n), s_sc.at[i, n], q_sc.at[i, n], gp((0, 1)))

    send(full.at[1, g, 0], full.at[1, g, 0], s_sx.at[2, 0], q_sx.at[2, 0], gp((2, 0)))
    over_y(g, s_s, q_s)
    arrived(full.at[1, far, 0], q_sx.at[2, 0])
    over_y(far, s_t, q_t)
    for n in range(2):
        gathered(g, q_s, n)
        for i in (1, 3):
            send(part(g, n), part(g, n), s_sx.at[i, n], q_sx.at[i, n], gp((i, 0)))
        to_core(0, g, n)
    for n in range(2):
        for i in (1, 3):
            k = go((4 - i, 0))
            arrived(part(k, n), q_sx.at[i, n])
            to_core(i, k, n)
        gathered(far, q_t, n)
        to_core(2, far, n)

    def second_products(k):
        @pl.when(k % 2 != q)
        def _():
            for n in range(2):
                arrived(part(k, n), q_sc.at[(x - k // 2 + 4) % 4, n])

        acc[k] += dot3((p2h[...], p2l[...]), split(whole(1, k))).reshape(14, 32, 128)

    ways = ((1, 0, 0), (-1, 1, 1))

    def hop(ring, hops, ss, qs, s, w, h, t):
        k = (c + s * (hops - t) + 8) % 8
        for j, (lo, hi) in enumerate(PIECES):
            here_in = ring.at[w, t, pl.ds(lo, hi - lo)]
            own = acc.at[k, pl.ds(7 * h + lo, hi - lo)]

            @pl.when(t == 0)
            def _():
                here_in[...] = own[...]

            @pl.when(t > 0)
            def _():
                arrived(here_in, qs.at[w, t, j])
                here_in[...] += own[...]

            pltpu.make_async_remote_copy(
                src_ref=here_in, dst_ref=ring.at[w, t + 1, pl.ds(lo, hi - lo)],
                send_sem=ss.at[w, t, j], recv_sem=qs.at[w, t + 1, j],
                device_id=zp(s + 8), device_id_type=MESH,
            ).start()

    def hop1(s, w, h, t):
        hop(ring1, 4, s_1, q_1, s, w, h, t)

    def hop2(s, w, h, t):
        hop(ring2, 3, s_2, q_2, s, w, 1 - h, t)

    def step(n, carry):
        second_products((c + jnp.where(n % 2 == 1, 4 - (n + 1) // 2, 4 + n // 2)) % 8)

        @pl.when(n == 0)
        def _():
            for s, w, h in ways:
                hop1(s, w, h, 0)

        @pl.when(jnp.logical_and(n % 2 == 1, n < 7))
        def _():
            hop2(*ways[0], (n - 1) // 2)

        @pl.when(jnp.logical_and(n % 2 == 0, n > 0))
        def _():
            hop2(*ways[1], (n - 2) // 2)

        @pl.when(jnp.logical_and(n % 2 == 0, n > 0))
        def _():
            for s, w, h in ways:
                hop1(s, w, h, n // 2)

        return carry

    lax.fori_loop(0, 8, step, 0)
    for i in range(2):
        for k in range(8):
            sol[i, :, 128 * k:128 * (k + 1)] = whole(i, k)
    rem[...] = rhs[2:] - acc[c]
    for ring, last, qs, other in ((ring2, 3, q_2, 1), (ring1, 4, q_1, 0)):
        for s, w, h in ways:
            for j, (lo, hi) in enumerate(PIECES):
                arrived(ring.at[w, last, pl.ds(lo, hi - lo)], qs.at[w, last, j])
                rem[pl.ds(7 * (h ^ other) + lo, hi - lo)] -= ring[w, last, lo:hi]
    for when, cp in sent:
        if when is None:
            cp.wait_send()
        else:
            pl.when(when)(cp.wait_send)
    for ring, hops, ss in ((ring1, 4, s_1), (ring2, 3, s_2)):
        for w in range(2):
            for t in range(hops):
                for j, (lo, hi) in enumerate(PIECES):
                    out = ring.at[w, t, pl.ds(lo, hi - lo)]
                    pltpu.make_async_remote_copy(
                        src_ref=out, dst_ref=out, send_sem=ss.at[w, t, j], recv_sem=ss.at[w, t, j],
                        device_id=zp(1), device_id_type=MESH,
                    ).wait_send()

    @pl.when(jnp.logical_and(moves, uses(g, c)))
    def _():
        here.wait_send()


def store(sol, rem, sol_out, rem_out, sem):
    copies = [
        pltpu.make_async_copy(src, dst, sem.at[i])
        for i, (src, dst) in enumerate(((sol.at[0], sol_out.at[0]), (sol.at[1], sol_out.at[1]), (rem, rem_out)))
    ]
    for copy in copies:
        copy.start()
    for copy in copies:
        copy.wait()


def shards(*args):
    vmem = pl.BlockSpec(memory_space=pltpu.VMEM)
    outside = pl.BlockSpec(memory_space=pltpu.HBM)

    def block(*shape):
        return pltpu.VMEM(shape, F32)

    def dma(*shape):
        return pltpu.SemaphoreType.DMA(shape)

    piece, matrix = (8, 32, 128), (8, 32, 256)
    outs = pl.pallas_call(
        kernel,
        out_shape=(
            jax.ShapeDtypeStruct((2, 256, 1024), F32),
            jax.ShapeDtypeStruct((14, 32, 128), F32),
        ),
        in_specs=[outside] * 4,
        out_specs=(vmem, vmem),
        scratch_shapes=[
            block(16, 32, 128), block(14, 32, 256), block(14, 32, 256), dma(6),
            block(*piece), block(*matrix), block(*matrix), block(*matrix), block(32, 128),
            block(*piece), block(*piece), block(*piece), block(*piece), block(*piece), block(*piece), block(*piece),
            block(2, 8, 8, 32, 128), block(8, 14, 32, 128),
            pltpu.VMEM((448, 256), BF16), pltpu.VMEM((448, 256), BF16),
            pltpu.VMEM((448, 256), BF16), pltpu.VMEM((448, 256), BF16),
            block(2, 5, 7, 32, 128), block(2, 4, 7, 32, 128),
            dma(3, 7), dma(3, 8), dma(1), dma(1), dma(8), dma(8), dma(8), dma(8),
            dma(8), dma(8), dma(4), dma(4), dma(4), dma(4),
            dma(8), dma(8), dma(8), dma(8), dma(8), dma(8), dma(8), dma(8),
            dma(8), dma(8), dma(4, 2), dma(4, 2), dma(4, 2), dma(4, 2), dma(2, 5, 2), dma(2, 5, 2), dma(2, 4, 2), dma(2, 4, 2),
        ],
        compiler_params=pltpu.CompilerParams(
            collective_id=0, has_side_effects=True, vmem_limit_bytes=32 * 1024 * 1024
        ),
        cost_estimate=pl.CostEstimate(flops=1500000000, bytes_accessed=5000000, transcendentals=0),
    )(*(pltpu.with_memory_space_constraint(v, pltpu.HBM) for v in args))
    return pl.pallas_call(
        store,
        out_shape=(
            jax.ShapeDtypeStruct((2, 256, 1024), F32),
            jax.ShapeDtypeStruct((14, 32, 128), F32),
        ),
        in_specs=[vmem] * 2,
        out_specs=(pl.BlockSpec(memory_space=pl.ANY),) * 2,
        scratch_shapes=[dma(3)],
    )(*(pltpu.with_memory_space_constraint(v, pltpu.VMEM) for v in outs))


def solution(mesh):
    return jax.shard_map(
        shards,
        mesh=mesh,
        in_specs=(
            P(None, "row", "col"),
            P(None, "row", "col"),
            P(None, "row", "col"),
            P(None, "row", "col"),
        ),
        out_specs=(P(None, "col", None), P(None, "row", "col")),
        check_vma=False,
    )
```

```python
import functools

import jax
import jax.numpy as jnp
from jax import lax
from jax.experimental import pallas as pl
from jax.experimental.pallas import tpu as pltpu
from jax.sharding import PartitionSpec as P

MESH = pl.DeviceIdType.MESH
F32 = jnp.float32
BF16 = jnp.bfloat16

NEAR = (1, 7, 2, 6, 3, 5, 4)
FAR = NEAR[::-1]
SLOT = (0, 1, 3, 5, 7, 6, 4, 2)
PARTS = ((0, 3), (3, 8))
PIECES = ((0, 4), (4, 7))
GROUP = ((2, 0), (2, 1), (1, 0), (3, 0), (1, 1), (3, 1), (0, 1))


def split(a):
    hi = a.astype(BF16)
    return hi, (a - hi.astype(F32)).astype(BF16)


def dot(a, b):
    return jnp.dot(a, b, preferred_element_type=F32)


def dot3(a, b):
    (ah, al), (bh, bl) = a, b
    return dot(ah, bh) + (dot(al, bh) + dot(ah, bl))


def kernel(
    rhs_h, pan1_h, pan2_h, inv_h, sol, rem,
    rhs, pan1, pan2, s_in, r, m0, m1, m2, r1t, pa, pa_in, pb, pb_in, u, pc, pc_in,
    full, acc, p1h, p1l, p2h, p2l, ring1, ring2,
    s_m, q_m, s_r1, q_r1, s_r, q_r, s_a, q_a, s_f, q_f, s_fx, q_fx, s_fc, q_fc,
    s_b, q_b, s_u, q_u, s_c, q_c, s_s, q_s, s_t, q_t, s_sx, q_sx, s_sc, q_sc, s_1, q_1, s_2, q_2,
):
    row = lax.axis_index("row")
    c = lax.axis_index("col")
    x, y, q = row // 16, (row // 2) % 8, row % 2
    g = 2 * x + q

    def dev(gg, yy, cc):
        return (((gg // 2) * 8 + yy) * 2 + gg % 2, cc)

    def zp(d):
        return dev(g, y, (c + d) % 8)

    def yp(d):
        return dev(g, (y + d) % 8, c)

    def go(e):
        return 2 * ((x + e[0]) % 4) + (q + e[1]) % 2

    def gp(e):
        return dev(go(e), y, c)

    sent = []

    def send(src, dst, ssem, rsem, to, when=None):
        cp = pltpu.make_async_remote_copy(
            src_ref=src, dst_ref=dst, send_sem=ssem, recv_sem=rsem, device_id=to, device_id_type=MESH
        )
        if when is None:
            cp.start()
        else:
            pl.when(when)(cp.start)
        sent.append((when, cp))

    def arrived(dst, rsem):
        pltpu.make_async_remote_copy(
            src_ref=dst, dst_ref=dst, send_sem=rsem, recv_sem=rsem, device_id=zp(1), device_id_type=MESH
        ).wait_recv()

    loads = [
        pltpu.make_async_copy(src, dst, s_in.at[i])
        for i, (src, dst) in enumerate((
            (rhs_h, rhs), (inv_h.at[0], m0.at[g]), (pan1_h.at[0], m1.at[g]), (inv_h.at[1], m2.at[g]),
            (pan2_h, pan2), (pan1_h.at[pl.ds(1, 14)], pan1),
        ))
    ]
    for load in loads:
        load.start()

    turned = dev(c, y, g)
    moves = g != c
    barrier = pltpu.get_barrier_semaphore()
    for d in NEAR:
        pl.semaphore_signal(barrier, inc=1, device_id=zp(d), device_id_type=MESH)
        pl.semaphore_signal(barrier, inc=1, device_id=yp(d), device_id_type=MESH)
    for e in GROUP:
        pl.semaphore_signal(barrier, inc=1, device_id=gp(e), device_id_type=MESH)
    for e in GROUP:
        pl.semaphore_signal(barrier, inc=1, device_id=dev(go(e), y, g), device_id_type=MESH)

    @pl.when(moves)
    def _():
        pl.semaphore_signal(barrier, inc=1, device_id=dev(g, y, g), device_id_type=MESH)

    for load in loads[:4]:
        load.wait()
    pl.semaphore_wait(barrier, 28 + jnp.where(moves, 1, 0))

    def uses(block, plane):
        return 2 * (block // 2) + y // 4 <= plane

    for d in FAR:
        send(rhs.at[0], r.at[g], s_r.at[d], q_r.at[g], dev(c, y, (c + d) % 8), uses(g, (c + d) % 8))
    here = pltpu.make_async_remote_copy(
        src_ref=rhs.at[0], dst_ref=r.at[g], send_sem=s_r.at[0], recv_sem=q_r.at[g],
        device_id=dev(c, y, c), device_id_type=MESH,
    )
    turn = pltpu.make_async_remote_copy(
        src_ref=rhs.at[1], dst_ref=r1t, send_sem=s_r1.at[0], recv_sem=q_r1.at[0], device_id=turned, device_id_type=MESH
    )

    @pl.when(jnp.logical_and(moves, uses(g, c)))
    def _():
        here.start()

    @pl.when(jnp.logical_not(moves))
    def _():
        r[g] = rhs[0]
        r1t[...] = rhs[1]

    for i, e in enumerate(GROUP):
        send(m0.at[g], m0.at[g], s_m.at[0, i], q_m.at[0, g], gp(e), uses(g, c))

    @pl.when(moves)
    def _():
        turn.start()

    for i, e in enumerate(GROUP):
        send(m1.at[g], m1.at[g], s_m.at[1, i], q_m.at[1, g], gp(e))
    for i, e in enumerate(GROUP):
        send(m2.at[g], m2.at[g], s_m.at[2, i], q_m.at[2, g], gp(e), uses(g, c))

    def split_panel(pan, hi, lo):
        h, l = split(pan[...].reshape(448, 256))
        hi[...] = h
        lo[...] = l

    for load in loads[4:]:
        load.wait()
    split_panel(pan2, p2h, p2l)

    def arrived_or_zero(buf, n, sem, needed):
        @pl.when(needed)
        def _():
            arrived(buf.at[n], sem)

        @pl.when(jnp.logical_not(needed))
        def _():
            buf[n] = jnp.zeros(buf.shape[1:], F32)

    for e in GROUP:
        arrived_or_zero(m0, go(e), q_m.at[0, go(e)], uses(go(e), c))
    m0s = split(m0[...].reshape(256, 256).T)
    for e in GROUP:
        arrived_or_zero(r, go(e), q_r.at[go(e)], uses(go(e), c))

    @pl.when(moves)
    def _():
        arrived_or_zero(r, g, q_r.at[g], uses(g, c))

    def whole(i, k):
        d = [(n - y + 8) % 8 for n in range(8)]
        at = [jnp.where(n == 0, 0, jnp.where(n <= 4, 2 * n - 1, 16 - 2 * n)) for n in d]
        return jnp.concatenate([full[i, k, n] for n in at], axis=0)

    def reduce_start(out, part, inn, ss, qs, peer, me):
        out[...] = part.reshape(8, 32, 128)
        for d in FAR:
            send(out.at[(me + d) % 8], inn.at[d], ss.at[d], qs.at[d], peer(d))

    def reduce_end(out, inn, qs, me):
        total = out[me]
        for d in NEAR:
            arrived(inn.at[d], qs.at[d])
            total = total + inn[d]
        return total

    reduce_start(pa, dot3(m0s, split(r[...].reshape(256, 128))), pa_in, s_a, q_a, yp, y)
    split_panel(pan1, p1h, p1l)
    full[0, g, 0] = reduce_end(pa, pa_in, q_a, y)
    for d in FAR:
        send(full.at[0, g, 0], full.at[0, g, SLOT[8 - d]], s_f.at[d], q_f.at[8 - d], yp(d))
    for e in GROUP:
        arrived(m1.at[go(e)], q_m.at[1, go(e)])
    m1s = split(m1[...].reshape(256, 256))
    for d in NEAR:
        arrived(full.at[0, g, SLOT[d]], q_f.at[d])

    reduce_start(pb, dot3(m1s, split(whole(0, g))), pb_in, s_b, q_b, zp, c)
    for i in (2, 1, 3):
        send(full.at[0, g], full.at[0, g], s_fx.at[i], q_fx.at[i], gp((i, 0)))
    send(full.at[0, g], full.at[0, g], s_fc.at[0], q_fc.at[0], gp((0, 1)))
    for e in GROUP:
        arrived_or_zero(m2, go(e), q_m.at[2, go(e)], uses(go(e), c))
    m2s = split(m2[...].reshape(256, 256).T)

    @pl.when(moves)
    def _():
        turn.wait()

    u[c] = r1t[...] - reduce_end(pb, pb_in, q_b, c)
    for d in FAR:
        send(u.at[c], u.at[c], s_u.at[d], q_u.at[c], zp(d), uses(c, (c + d) % 8))
    for i in (1, 3, 2):
        came = go((4 - i, 0))
        arrived(full.at[0, came], q_fx.at[i])
        send(full.at[0, came], full.at[0, came], s_fc.at[i], q_fc.at[i], gp((0, 1)))
    for d in NEAR:
        n = (c + d) % 8
        arrived_or_zero(u, n, q_u.at[n], uses(n, c))

    reduce_start(pc, dot3(m2s, split(u[...].reshape(256, 128))), pc_in, s_c, q_c, yp, y)
    for i in range(4):
        arrived(full.at[0, go(((4 - i) % 4, 1))], q_fc.at[i])

    def first_products(j, carry):
        b = jnp.concatenate([whole(0, 2 * j), whole(0, 2 * j + 1)], axis=1)
        o = dot3((p1h[...], p1l[...]), split(b))
        acc[2 * j] = o[:, :128].reshape(14, 32, 128)
        acc[2 * j + 1] = o[:, 128:].reshape(14, 32, 128)
        return carry

    lax.fori_loop(0, 4, first_products, 0)
    full[1, g, 0] = reduce_end(pc, pc_in, q_c, y)

    far = go((2, 0))

    def part(k, n):
        lo, hi = PARTS[n]
        return full.at[1, k, pl.ds(lo, hi - lo)]

    def over_y(k, ss, qs):
        for d in FAR:
            send(full.at[1, k, 0], full.at[1, k, SLOT[8 - d]], ss.at[d], qs.at[8 - d], yp(d))

    def gathered(k, qs, n):
        lo, hi = PARTS[n]
        for d in NEAR:
            if lo <= SLOT[d] < hi:
                arrived(full.at[1, k, SLOT[d]], qs.at[d])

    def to_core(i, k, n):
        send(part(k, n), part(k, n), s_sc.at[i, n], q_sc.at[i, n], gp((0, 1)))

    send(full.at[1, g, 0], full.at[1, g, 0], s_sx.at[2, 0], q_sx.at[2, 0], gp((2, 0)))
    over_y(g, s_s, q_s)
    arrived(full.at[1, far, 0], q_sx.at[2, 0])
    over_y(far, s_t, q_t)
    for n in range(2):
        gathered(g, q_s, n)
        for i in (1, 3):
            send(part(g, n), part(g, n), s_sx.at[i, n], q_sx.at[i, n], gp((i, 0)))
        to_core(0, g, n)
    for n in range(2):
        for i in (1, 3):
            k = go((4 - i, 0))
            arrived(part(k, n), q_sx.at[i, n])
            to_core(i, k, n)
        gathered(far, q_t, n)
        to_core(2, far, n)

    def second_products(k):
        @pl.when(k % 2 != q)
        def _():
            for n in range(2):
                arrived(part(k, n), q_sc.at[(x - k // 2 + 4) % 4, n])

        acc[k] += dot3((p2h[...], p2l[...]), split(whole(1, k))).reshape(14, 32, 128)

    ways = ((1, 0, 0), (-1, 1, 1))

    def hop(ring, hops, ss, qs, s, w, h, t):
        k = (c + s * (hops - t) + 8) % 8
        for j, (lo, hi) in enumerate(PIECES):
            here_in = ring.at[w, t, pl.ds(lo, hi - lo)]
            own = acc.at[k, pl.ds(7 * h + lo, hi - lo)]

            @pl.when(t == 0)
            def _():
                here_in[...] = own[...]

            @pl.when(t > 0)
            def _():
                arrived(here_in, qs.at[w, t, j])
                here_in[...] += own[...]

            pltpu.make_async_remote_copy(
                src_ref=here_in, dst_ref=ring.at[w, t + 1, pl.ds(lo, hi - lo)],
                send_sem=ss.at[w, t, j], recv_sem=qs.at[w, t + 1, j],
                device_id=zp(s + 8), device_id_type=MESH,
            ).start()

    def hop1(s, w, h, t):
        hop(ring1, 4, s_1, q_1, s, w, h, t)

    def hop2(s, w, h, t):
        hop(ring2, 3, s_2, q_2, s, w, 1 - h, t)

    def step(n, carry):
        second_products((c + jnp.where(n % 2 == 1, 4 - (n + 1) // 2, 4 + n // 2)) % 8)

        @pl.when(n == 0)
        def _():
            for s, w, h in ways:
                hop1(s, w, h, 0)

        @pl.when(n == 1)
        def _():
            hop2(*ways[0], 0)

        @pl.when(n == 2)
        def _():
            hop2(*ways[1], 0)

        @pl.when(jnp.logical_or(n == 4, n == 6))
        def _():
            t = n // 2 - 1
            for s, w, h in ways:
                hop1(s, w, h, t)
            for s, w, h in ways:
                hop2(s, w, h, t)

        @pl.when(n == 7)
        def _():
            for s, w, h in ways:
                hop1(s, w, h, 3)

        return carry

    lax.fori_loop(0, 8, step, 0)
    for i in range(2):
        for k in range(8):
            sol[i, :, 128 * k:128 * (k + 1)] = whole(i, k)
    rem[...] = rhs[2:] - acc[c]
    for ring, last, qs, other in ((ring2, 3, q_2, 1), (ring1, 4, q_1, 0)):
        for s, w, h in ways:
            for j, (lo, hi) in enumerate(PIECES):
                arrived(ring.at[w, last, pl.ds(lo, hi - lo)], qs.at[w, last, j])
                rem[pl.ds(7 * (h ^ other) + lo, hi - lo)] -= ring[w, last, lo:hi]
    for when, cp in sent:
        if when is None:
            cp.wait_send()
        else:
            pl.when(when)(cp.wait_send)
    for ring, hops, ss in ((ring1, 4, s_1), (ring2, 3, s_2)):
        for w in range(2):
            for t in range(hops):
                for j, (lo, hi) in enumerate(PIECES):
                    out = ring.at[w, t, pl.ds(lo, hi - lo)]
                    pltpu.make_async_remote_copy(
                        src_ref=out, dst_ref=out, send_sem=ss.at[w, t, j], recv_sem=ss.at[w, t, j],
                        device_id=zp(1), device_id_type=MESH,
                    ).wait_send()

    @pl.when(jnp.logical_and(moves, uses(g, c)))
    def _():
        here.wait_send()


def store(sol, rem, sol_out, rem_out, sem):
    copies = [
        pltpu.make_async_copy(src, dst, sem.at[i])
        for i, (src, dst) in enumerate(((sol.at[0], sol_out.at[0]), (sol.at[1], sol_out.at[1]), (rem, rem_out)))
    ]
    for copy in copies:
        copy.start()
    for copy in copies:
        copy.wait()


def shards(*args):
    vmem = pl.BlockSpec(memory_space=pltpu.VMEM)
    outside = pl.BlockSpec(memory_space=pltpu.HBM)

    def block(*shape):
        return pltpu.VMEM(shape, F32)

    def dma(*shape):
        return pltpu.SemaphoreType.DMA(shape)

    piece, matrix = (8, 32, 128), (8, 32, 256)
    outs = pl.pallas_call(
        kernel,
        out_shape=(
            jax.ShapeDtypeStruct((2, 256, 1024), F32),
            jax.ShapeDtypeStruct((14, 32, 128), F32),
        ),
        in_specs=[outside] * 4,
        out_specs=(vmem, vmem),
        scratch_shapes=[
            block(16, 32, 128), block(14, 32, 256), block(14, 32, 256), dma(6),
            block(*piece), block(*matrix), block(*matrix), block(*matrix), block(32, 128),
            block(*piece), block(*piece), block(*piece), block(*piece), block(*piece), block(*piece), block(*piece),
            block(2, 8, 8, 32, 128), block(8, 14, 32, 128),
            pltpu.VMEM((448, 256), BF16), pltpu.VMEM((448, 256), BF16),
            pltpu.VMEM((448, 256), BF16), pltpu.VMEM((448, 256), BF16),
            block(2, 5, 7, 32, 128), block(2, 4, 7, 32, 128),
            dma(3, 7), dma(3, 8), dma(1), dma(1), dma(8), dma(8), dma(8), dma(8),
            dma(8), dma(8), dma(4), dma(4), dma(4), dma(4),
            dma(8), dma(8), dma(8), dma(8), dma(8), dma(8), dma(8), dma(8),
            dma(8), dma(8), dma(4, 2), dma(4, 2), dma(4, 2), dma(4, 2), dma(2, 5, 2), dma(2, 5, 2), dma(2, 4, 2), dma(2, 4, 2),
        ],
        compiler_params=pltpu.CompilerParams(
            collective_id=0, has_side_effects=True, vmem_limit_bytes=32 * 1024 * 1024
        ),
        cost_estimate=pl.CostEstimate(flops=1500000000, bytes_accessed=5000000, transcendentals=0),
    )(*(pltpu.with_memory_space_constraint(v, pltpu.HBM) for v in args))
    return pl.pallas_call(
        store,
        out_shape=(
            jax.ShapeDtypeStruct((2, 256, 1024), F32),
            jax.ShapeDtypeStruct((14, 32, 128), F32),
        ),
        in_specs=[vmem] * 2,
        out_specs=(pl.BlockSpec(memory_space=pl.ANY),) * 2,
        scratch_shapes=[dma(3)],
    )(*(pltpu.with_memory_space_constraint(v, pltpu.VMEM) for v in outs))


def solution(mesh):
    return jax.shard_map(
        shards,
        mesh=mesh,
        in_specs=(
            P(None, "row", "col"),
            P(None, "row", "col"),
            P(None, "row", "col"),
            P(None, "row", "col"),
        ),
        out_specs=(P(None, "col", None), P(None, "row", "col")),
        check_vma=False,
    )
```
